512 devices in a mesh: dp: 16 (over z, core), expert: 8 (over y), tensor: 4 (over x).
Axes of the slice: x: 4, y: 8, z: 8, core: 2. Of those that a mesh axis runs over, the one named last changes fastest.
Arguments:
- expert_out: bfloat16 [8, 24576, 3072], P('expert', 'dp', 'tensor'), parts along dimension 1, may hold values from -6 to 6
- kept_blocks: int32 [8, 192], P('expert', 'dp'), parts along dimension 1, may hold values from 0 to 1, as said below
- expert_ids: int32 [65536, 2], P(('dp', 'expert', 'tensor')), parts along dimension 0, may hold values from 0 to 7, all different within a row; in each aligned block of 128 rows (0 to 127, 128 to 255, ...) at most 48 rows name the same one
- gate_levels: int32 [65536, 2], P(('dp', 'expert', 'tensor')), parts along dimension 0, may hold values from 16 to 240
- norm_gain: bfloat16 [3072], replicated, may hold values from 0.099609375 to 1.8984375
- qkv_weight: bfloat16 [3072, 4096], P('expert', 'tensor'), may hold values from -0.109375 to 0.109375
Outputs:
- qkv: bfloat16 [65536, 4096], P(('dp', 'expert'), 'tensor'), parts along dimension 0
The draws below stay inside these ranges and needn't reach their ends.
There are 16 independent parts, one for each index of `dp`. The reference program is written for one: setup_inputs(seed, part) draws one part's arguments, and reference() takes and returns one part's arrays. A program takes and returns all parts, laid end to end along the dimension named above; an argument that names none is the same for every part. Nothing has to cross between parts.
Inputs may be any that keep to these rules, and one draw needn't show every extreme that they name: `kept_blocks`: each expert keeps a leading run of one or more of its 12 blocks; in every draw some expert keeps all of them. `expert_ids`: the two experts of a token differ; among the tokens of one owner device (aligned blocks of 128 rows) each expert is named at most 48 times, a bound that some block reaches.
All inputs are finite; a program needn't handle non-finite values.
Results may differ from the reference program's by a relative error of at most 0.0049.
Values may be sent and summed in bfloat16 or wider, within the bound.
No kernel may reach another device: no remote copies, remote signals or barrier semaphores. Data moves between devices by JAX's collectives and lax.ppermute only.
A program may use at most 64 MiB of HBM per device.

```python
import math
import jax
import jax.numpy as jnp
import numpy as np
from jax import lax

D = 3072
QKV = 4096
TOK_DEV = 128
EXPERTS = 8
SLOT = 48
NBLK = 12
ROWS = 1536
TOKENS = 4096
N_EXPERT = 8
N_TENSOR = 4


def draw_kept_blocks(key, part):
    key = jax.random.fold_in(key, 7)
    first, second = jax.random.split(key)
    lowest = max(1, NBLK - 3)
    counts = jax.random.randint(first, (EXPERTS,), lowest, NBLK + 1)
    fullest = jax.random.randint(second, (), 0, EXPERTS)
    counts = jnp.where(jnp.arange(EXPERTS) == fullest, NBLK, counts)
    return (jnp.arange(NBLK)[None, :] < counts[:, None]).astype(jnp.int32)


def with_ends(values, rng, low, high):
    shape = values.shape
    index_at = [jax.random.randint(jax.random.fold_in(rng, axis), (), 0, shape[axis]) for axis in range(len(shape))]
    values = values.at[tuple(index_at)].set(low)
    longest = shape.index(max(shape))
    index_at[longest] = (index_at[longest] + 1) % shape[longest]
    return values.at[tuple(index_at)].set(high)


def shard_levels(key, extent, cuts, smallest, largest):
    level = 1.0
    for position, blocks in cuts:
        draws = jax.random.uniform(jax.random.fold_in(jax.random.fold_in(key, 6), position), (blocks,), jnp.float32, smallest / len(cuts), largest / len(cuts))
        level = level * jnp.repeat(jnp.exp(draws), extent[position] // blocks).reshape((-1,) + (1,) * (len(extent) - 1 - position))
    return level


def routed_block(own_key, own, number, rows, number_of, top, limit, skew):
    ranking = jax.random.permutation(own_key, number_of)
    heavy_load, usual = load_shares(number_of, rows * top, limit, skew, True), load_shares(number_of, rows * top, limit, skew, False)
    places = jnp.arange(number_of)

    def named(tallies, turn):
        used = int((tallies > 0).sum())
        fixed = max(1, used // 4)
        shifted = fixed + (places - fixed + turn * (used - fixed)) % max(1, number_of - fixed)
        return jnp.zeros((number_of,), jnp.int32).at[ranking[jnp.where(places < fixed, places, shifted)]].set(jnp.asarray(tallies, jnp.int32))

    tallies = jnp.where(number % 4 == 0, named(heavy_load, number // 4), named(usual, number - number // 4 - 1))
    mixed = jax.random.permutation(jax.random.fold_in(own, 3), number_of)
    source_of, sink = mixed[0:number_of // 2 * 2:2], mixed[1:number_of // 2 * 2:2]
    slack = jnp.minimum(tallies[source_of] - 1, limit - tallies[sink]) // 2
    slack = jnp.where((source_of == ranking[0]) | (sink == ranking[0]) | (tallies[sink] == 0), 0, jnp.maximum(slack, 0))
    shifted = jax.random.randint(jax.random.fold_in(own, 4), (number_of // 2,), 0, 1 << 20) % (slack + 1)
    tallies = tallies.at[source_of].add(-shifted).at[sink].add(shifted)
    members = jnp.searchsorted(jnp.cumsum(tallies), jnp.arange(rows * top), side="right").astype(jnp.int32)
    table = members.reshape(top, rows).T
    table = table[jax.random.permutation(jax.random.fold_in(own, 1), rows)]
    turn = jax.random.randint(jax.random.fold_in(own, 2), (rows, 1), 0, top)
    return jnp.take_along_axis(table, (jnp.arange(top)[None, :] + turn) % top, axis=1)


def load_shares(amount, total, reach, lean, full):
    weights = [(1 << 20) // math.isqrt(standing ** lean) + 1 for standing in range(1, amount + 1)]
    largest = reach if full else min(reach, max(-(-total // amount), total * weights[0] // sum(weights)))
    least = 1 if total - largest >= amount - 1 else 0
    given, spare = [largest] + [least] * (amount - 1), total - largest - least * (amount - 1)
    while spare > 0:
        movable = [i for i in range(1, amount) if given[i] < largest] or [i for i in range(1, amount) if given[i] < reach]
        mass, remaining = sum([weights[i] for i in movable]), spare
        for i in movable:
            extra = min(reach - given[i], max(1, remaining * weights[i] // mass), spare)
            given[i] = given[i] + extra
            spare = spare - extra
    return np.array(given)


def scatter_about(rng, dims, spread, reach, shards=(), held_as=jnp.bfloat16):
    values = jax.random.normal(rng, dims, jnp.float32) * spread
    if len(shards) > 0:
        values = shard_levels(rng, dims, shards, -0.22, 0.18) * values
    return jnp.clip(values, min=-reach, max=reach).astype(held_as)


def setup_inputs(seed: int = 0, part: int = 0) -> dict:
    key_of = jax.random.split(jax.random.key(seed), 7)
    part_keys = jax.random.split(jax.random.fold_in(key_of[6], part), 7)
    expert_out = scatter_about(part_keys[0], (EXPERTS, ROWS, D), 1.0, 6.0, ((0, 8), (2, 4)))
    kept_blocks = draw_kept_blocks(jax.random.fold_in(jax.random.fold_in(key_of[6], part), 71), part)
    expert_ids_keys = jax.random.split(jax.random.fold_in(part_keys[2], 1), TOKENS // TOK_DEV)
    expert_ids_turns = jax.random.permutation(jax.random.fold_in(part_keys[2], 3), TOKENS // TOK_DEV)
    expert_ids = jax.vmap(lambda own, number: routed_block(jax.random.fold_in(part_keys[2], 2), own, number, TOK_DEV, EXPERTS, 2, SLOT, 2))(expert_ids_keys, expert_ids_turns).reshape((TOKENS, 2))
    gate_levels = with_ends(jax.random.randint(part_keys[3], (TOKENS, 2), 16, 241), jax.random.fold_in(part_keys[3], 1), 16, 240).astype(jnp.int32)
    norm_gain = jnp.clip(1.0 + 0.18 * jax.random.normal(key_of[4], (D,), jnp.float32), 0.099609375, 1.8984375).astype(jnp.bfloat16)
    qkv_weight = scatter_about(key_of[5], (D, QKV), D ** -0.5, 0.109375, ((0, 8), (1, 4)))
    return dict(expert_out=expert_out, kept_blocks=kept_blocks, expert_ids=expert_ids, gate_levels=gate_levels, norm_gain=norm_gain, qkv_weight=qkv_weight)


def slot_ranks(expert_ids):
    one_hot = (expert_ids[:, :, None] == jnp.arange(EXPERTS)[None, None, :]).astype(jnp.int32)
    per_token = lax.optimization_barrier(jnp.sum(one_hot, axis=1)).reshape(-1, TOK_DEV, EXPERTS)
    earlier = (jnp.cumsum(per_token, axis=1) - per_token).reshape(-1, EXPERTS)
    return lax.optimization_barrier(jnp.sum(earlier[:, None, :] * one_hot, axis=-1)).astype(jnp.int32)

def reference(expert_out, kept_blocks, expert_ids, gate_levels, norm_gain, qkv_weight):
    devices = N_EXPERT * N_TENSOR
    block_of = jnp.arange(ROWS) // (4 * devices)
    row_mask = kept_blocks[:, block_of].astype(jnp.bfloat16)
    outputs = expert_out * row_mask[:, :, None]
    slot = slot_ranks(expert_ids)
    owner = (jnp.arange(TOKENS) // TOK_DEV).astype(jnp.int32)[:, None]
    row_index = slot * devices + owner
    picked = outputs[expert_ids, row_index].astype(jnp.float32)
    weights = gate_levels.astype(jnp.float32) / 256.0
    combined = lax.optimization_barrier(jnp.sum(weights[:, :, None] * picked, axis=1))
    scale = jax.lax.rsqrt(lax.optimization_barrier(jnp.mean(combined * combined, axis=-1, keepdims=True)) + 1e-05)
    normed = (combined * scale * norm_gain.astype(jnp.float32)).astype(jnp.bfloat16)
    return jnp.dot(normed, qkv_weight, preferred_element_type=jnp.float32).astype(jnp.bfloat16)
```

```python
import functools

import jax
import jax.numpy as jnp
from jax import lax
from jax.experimental import pallas as pl
from jax.experimental.pallas import tpu as pltpu
from jax.sharding import PartitionSpec as P

F32 = jnp.float32
BF16 = jnp.bfloat16
VMEM_LIMIT = 48 * 1024 * 1024


def select_kernel(experts, slots, ids_ref, sel_ref):
    tok = ids_ref.shape[1]
    cols = experts * slots
    row = lax.broadcasted_iota(jnp.int32, (tok, tok), 0)
    col = lax.broadcasted_iota(jnp.int32, (tok, tok), 1)
    before = (col < row).astype(F32).astype(BF16)
    lane = lax.broadcasted_iota(jnp.int32, (tok, 128), 1)
    place = lax.broadcasted_iota(jnp.int32, (tok, cols), 1)
    for q in range(ids_ref.shape[0]):
        both = ids_ref[q]
        hot = [(lane == both[:, k : k + 1]).astype(F32) for k in range(2)]
        earlier = jnp.dot(before, (hot[0] + hot[1]).astype(BF16), preferred_element_type=F32)
        total = jnp.zeros((tok, cols), F32)
        for k in range(2):
            slot = jnp.sum(earlier * hot[k], axis=1, keepdims=True).astype(jnp.int32)
            target = both[:, k : k + 1] * slots + slot
            share = both[:, 2 + k : 3 + k].astype(F32) / 256.0
            total = total + jnp.where(place == target, share, 0.0)
        sel_ref[q] = total.astype(BF16)


def select(ids, experts, slots):
    owners, tok, _ = ids.shape
    return pl.pallas_call(
        functools.partial(select_kernel, experts, slots),
        out_shape=jax.ShapeDtypeStruct((owners, tok, experts * slots), BF16),
    )(ids)


def combine_kernel(sel_ref, rows_ref, gain_ref, out_ref):
    experts, owners, slots, width = rows_ref.shape
    tok = sel_ref.shape[1]
    for q in range(owners):
        rows = rows_ref[:, q].reshape(experts * slots, width)
        total = jnp.dot(sel_ref[q], rows, preferred_element_type=F32)
        out_ref[pl.ds(q * tok, tok), :] = (total * gain_ref[...]).astype(BF16)


def combine(sel, rows, gain):
    owners, tok, _ = sel.shape
    return pl.pallas_call(
        combine_kernel,
        out_shape=jax.ShapeDtypeStruct((owners * tok, rows.shape[3]), BF16),
    )(sel, rows, gain)


def project_kernel(width, place_ref, own_ref, one_ref, two_ref, three_ref, w_ref, inv_ref, *rest):
    out_ref, scale_ref = rest[-2:]
    blocks = (own_ref, one_ref, two_ref, three_ref)

    @pl.when(pl.program_id(0) == 0)
    def _():
        total = jnp.zeros(scale_ref.shape, F32)
        for k, block in enumerate(blocks):
            plain = block[...].astype(F32) * inv_ref[place_ref[k]]
            total = total + jnp.sum(plain * plain, axis=1, keepdims=True)
        scale_ref[...] = lax.rsqrt(total / width + 1e-05)

    acc = jnp.dot(own_ref[...], w_ref[place_ref[0]], preferred_element_type=F32)
    for k in range(1, 4):
        acc = acc + jnp.dot(blocks[k][...], w_ref[place_ref[k]], preferred_element_type=F32)
    out_ref[...] = (acc * scale_ref[...]).astype(BF16)


def project(place, blocks, weight, inv_gain, total_rows, row_block, into=None):
    rows, quarter = blocks[0].shape
    parts, _, columns = weight.shape
    tile = 256
    whole = pl.BlockSpec((rows, quarter), lambda j, p: (0, 0))
    in_specs = [whole] * 4 + [
        pl.BlockSpec((parts, quarter, tile), lambda j, p: (0, 0, j)),
        pl.BlockSpec((parts, 1, quarter), lambda j, p: (0, 0, 0)),
    ]
    args = [place, *blocks, weight, inv_gain]
    aliases = {}
    if into is not None:
        in_specs.append(pl.BlockSpec(memory_space=pl.ANY))
        aliases = {len(args): 0}
        args.append(into)
    return pl.pallas_call(
        functools.partial(project_kernel, parts * quarter),
        out_shape=jax.ShapeDtypeStruct((total_rows, columns), BF16),
        grid_spec=pltpu.PrefetchScalarGridSpec(
            num_scalar_prefetch=1,
            grid=(columns // tile,),
            in_specs=in_specs,
            out_specs=pl.BlockSpec((rows, tile), lambda j, p: (row_block, j)),
            scratch_shapes=[pltpu.VMEM((rows, 1), F32)],
        ),
        input_output_aliases=aliases,
        compiler_params=pltpu.CompilerParams(vmem_limit_bytes=VMEM_LIMIT),
    )(*args)


def local(expert_out, kept_blocks, expert_ids, gate_levels, norm_gain, qkv_weight):
    parts = lax.axis_size("dp")
    experts = lax.axis_size("expert")
    tensors = lax.axis_size("tensor")
    part, mine, quarter_of = (lax.axis_index(a) for a in ("dp", "expert", "tensor"))
    devices = experts * tensors
    rows, quarter = expert_out.shape[1:]
    slots = rows // devices
    tok = expert_ids.shape[0]

    share = qkv_weight.shape[0] // parts
    columns = qkv_weight.shape[1]
    w = lax.dynamic_slice(qkv_weight, (part * share, 0), (share, columns))
    w = w.reshape(1, 1, 1, share, columns)
    for axis, step in enumerate((4, 2, 1)):
        other = lax.ppermute(w, "expert", [(i, i ^ step) for i in range(experts)])
        upper = (mine & step) != 0
        w = jnp.concatenate([jnp.where(upper, other, w), jnp.where(upper, w, other)], axis=axis)
    w = lax.all_gather(w.reshape(experts * share, columns), "dp", axis=0, tiled=True)
    weight = (
        w.reshape(parts, experts, share, columns)
        .transpose(1, 0, 2, 3)
        .reshape(tensors, quarter, columns)
    )

    mask = jnp.repeat(kept_blocks[0], 4 * devices).astype(BF16)
    masked = (expert_out[0] * mask[:, None]).reshape(slots, experts, tensors, quarter)
    outgoing = masked.transpose(1, 2, 0, 3)

    ids = lax.all_gather(jnp.concatenate([expert_ids, gate_levels], axis=1), "tensor")
    sel = select(ids, experts, slots)

    gain = norm_gain.astype(F32)
    inv_gain = (1.0 / gain).reshape(tensors, 1, quarter)
    own_gain = lax.dynamic_slice(gain, (quarter_of * quarter,), (quarter,)).reshape(1, quarter)
    place = (quarter_of - jnp.arange(tensors, dtype=jnp.int32)) % tensors

    out = None
    for lo, hi in ((0, 3), (3, 4)):
        arrived = lax.all_to_all(outgoing[:, lo:hi], "expert", 0, 0, tiled=True)
        own = combine(sel[lo:hi], arrived, own_gain)
        blocks = [own] + [
            lax.ppermute(own, "tensor", [(i, (i + k) % tensors) for i in range(tensors)])
            for k in range(1, tensors)
        ]
        out = project(place, blocks, weight, inv_gain, tensors * tok, lo // (hi - lo), out)
    return out


def solution(mesh):
    in_specs = (
        P("expert", "dp", "tensor"),
        P("expert", "dp"),
        P(("dp", "expert", "tensor"), None),
        P(("dp", "expert", "tensor"), None),
        P(),
        P("expert", "tensor"),
    )
    out_specs = P(("dp", "expert"), "tensor")
    return jax.shard_map(local, mesh=mesh, in_specs=in_specs, out_specs=out_specs, check_vma=False)
```

```python
import functools

import jax
import jax.numpy as jnp
from jax import lax
from jax.experimental import pallas as pl
from jax.experimental.pallas import tpu as pltpu
from jax.sharding import PartitionSpec as P

F32 = jnp.float32
BF16 = jnp.bfloat16
VMEM_LIMIT = 48 * 1024 * 1024


def pack_kernel(kept_ref, rows_ref, *out_refs):
    slots, owners, width = rows_ref.shape
    per_block = 4
    step = pl.program_id(0)
    row = lax.broadcasted_iota(jnp.int32, (slots * owners, slots * owners), 0)
    col = lax.broadcasted_iota(jnp.int32, (slots * owners, slots * owners), 1)
    row_slot = lax.rem(row, slots)
    same = (lax.div(row, slots) == lax.rem(col, owners)) & (row_slot == lax.div(col, owners))
    block = lax.div(row_slot, per_block)
    kept = jnp.zeros(row.shape, jnp.int32)
    for b in range(slots // per_block):
        kept = jnp.where(block == b, kept_ref[step * (slots // per_block) + b], kept)
    move = (same & (kept != 0)).astype(F32).astype(BF16)
    moved = jnp.dot(
        move, rows_ref[...].reshape(slots * owners, width), preferred_element_type=F32
    ).astype(BF16)
    experts = out_refs[0].shape[0]
    moved = moved.reshape(experts, owners // experts, slots, width)
    at = 0
    for ref in out_refs:
        ref[...] = moved[:, at : at + ref.shape[1]]
        at += ref.shape[1]


def pack(kept, rows, experts, pieces):
    slots, owners, width = rows.shape
    step = 16
    return pl.pallas_call(
        pack_kernel,
        out_shape=[jax.ShapeDtypeStruct((experts, n, slots, width), BF16) for n in pieces],
        grid_spec=pltpu.PrefetchScalarGridSpec(
            num_scalar_prefetch=1,
            grid=(slots // step,),
            in_specs=[pl.BlockSpec((step, owners, width), lambda j, k: (j, 0, 0))],
            out_specs=[pl.BlockSpec((experts, n, step, width), lambda j, k: (0, 0, j, 0)) for n in pieces],
        ),
        compiler_params=pltpu.CompilerParams(vmem_limit_bytes=60 * 1024 * 1024),
    )(kept, rows)


def select_kernel(experts, slots, ids_ref, sel_ref):
    tok = ids_ref.shape[1]
    cols = experts * slots
    row = lax.broadcasted_iota(jnp.int32, (tok, tok), 0)
    col = lax.broadcasted_iota(jnp.int32, (tok, tok), 1)
    before = (col < row).astype(F32).astype(BF16)
    lane = lax.broadcasted_iota(jnp.int32, (tok, 128), 1)
    place = lax.broadcasted_iota(jnp.int32, (tok, cols), 1)
    for q in range(ids_ref.shape[0]):
        both = ids_ref[q]
        hot = [(lane == both[:, k : k + 1]).astype(F32) for k in range(2)]
        earlier = jnp.dot(before, (hot[0] + hot[1]).astype(BF16), preferred_element_type=F32)
        total = jnp.zeros((tok, cols), F32)
        for k in range(2):
            slot = jnp.sum(earlier * hot[k], axis=1, keepdims=True).astype(jnp.int32)
            target = both[:, k : k + 1] * slots + slot
            share = both[:, 2 + k : 3 + k].astype(F32) / 256.0
            total = total + jnp.where(place == target, share, 0.0)
        sel_ref[q] = total.astype(BF16)


def select(ids, experts, slots):
    owners, tok, _ = ids.shape
    return pl.pallas_call(
        functools.partial(select_kernel, experts, slots),
        out_shape=jax.ShapeDtypeStruct((owners, tok, experts * slots), BF16),
    )(ids)


def combine_kernel(sel_ref, rows_ref, gain_ref, out_ref):
    experts, owners, slots, width = rows_ref.shape
    tok = sel_ref.shape[1]
    for q in range(owners):
        rows = rows_ref[:, q].reshape(experts * slots, width)
        total = jnp.dot(sel_ref[q], rows, preferred_element_type=F32)
        out_ref[pl.ds(q * tok, tok), :] = (total * gain_ref[...]).astype(BF16)


def combine(sel, first, rows, gain):
    tok, cols = sel.shape[1:]
    experts, owners, slots, width = rows.shape
    return pl.pallas_call(
        combine_kernel,
        out_shape=jax.ShapeDtypeStruct((owners * tok, width), BF16),
        grid=(1,),
        in_specs=[
            pl.BlockSpec((owners, tok, cols), lambda i: (first // owners, 0, 0)),
            pl.BlockSpec(rows.shape, lambda i: (0, 0, 0, 0)),
            pl.BlockSpec(gain.shape, lambda i: (0, 0)),
        ],
        out_specs=pl.BlockSpec((owners * tok, width), lambda i: (0, 0)),
        cost_estimate=pl.CostEstimate(flops=45625000000, bytes_accessed=0, transcendentals=0),
        compiler_params=pltpu.CompilerParams(vmem_limit_bytes=VMEM_LIMIT),
    )(sel, rows, gain)


def project_kernel(width, pieces, place_ref, w_ref, inv_ref, *refs):
    blocks = [refs[4 * i : 4 * i + 4] for i in range(pieces)]
    out_ref, scale_ref = refs[-2:]
    half = pl.program_id(0)

    @pl.when(half == 0)
    def _():
        at = 0
        for piece in blocks:
            rows = piece[0].shape[0]
            total = jnp.zeros((rows, 1), F32)
            for k, block in enumerate(piece):
                plain = block[...].astype(F32) * inv_ref[place_ref[1 + k]]
                total = total + jnp.sum(plain * plain, axis=1, keepdims=True)
            scale_ref[pl.ds(at, rows), :] = lax.rsqrt(total / width + 1e-05)
            at += rows

    shards, _, share, _ = w_ref.shape
    at = 0
    for piece in blocks:
        rows = piece[0].shape[0]
        acc = None
        for k, block in enumerate(piece):
            for i in range(2):
                shard = 2 * place_ref[1 + k] + i
                plane = lax.rem(shard - place_ref[0] + 4 * half + shards, shards)
                term = jnp.dot(
                    block[:, i * share : (i + 1) * share], w_ref[plane, 0], preferred_element_type=F32
                )
                acc = term if acc is None else acc + term
        out_ref[pl.ds(at, rows), :] = (acc * scale_ref[pl.ds(at, rows), :]).astype(BF16)
        at += rows


def project(place, pieces, weight, inv_gain):
    shards, halves, share, columns = weight.shape
    rows = sum(piece[0].shape[0] for piece in pieces)
    in_specs = [
        pl.BlockSpec((shards, 1, share, columns), lambda j, p: (0, j, 0, 0)),
        pl.BlockSpec(inv_gain.shape, lambda j, p: (0, 0, 0)),
    ]
    args = [place, weight, inv_gain]
    for piece in pieces:
        for block in piece:
            in_specs.append(pl.BlockSpec(block.shape, lambda j, p: (0, 0)))
            args.append(block)
    return pl.pallas_call(
        functools.partial(project_kernel, shards * share, len(pieces)),
        out_shape=jax.ShapeDtypeStruct((rows, halves * columns), BF16),
        grid_spec=pltpu.PrefetchScalarGridSpec(
            num_scalar_prefetch=1,
            grid=(halves,),
            in_specs=in_specs,
            out_specs=pl.BlockSpec((rows, columns), lambda j, p: (0, j)),
            scratch_shapes=[pltpu.VMEM((rows, 1), F32)],
        ),
        compiler_params=pltpu.CompilerParams(vmem_limit_bytes=VMEM_LIMIT),
    )(*args)


def local(expert_out, kept_blocks, expert_ids, gate_levels, norm_gain, qkv_weight):
    parts = lax.axis_size("dp")
    experts = lax.axis_size("expert")
    tensors = lax.axis_size("tensor")
    part, mine, quarter_of = (lax.axis_index(a) for a in ("dp", "expert", "tensor"))
    devices = experts * tensors
    rows, quarter = expert_out.shape[1:]
    slots = rows // devices
    tok = expert_ids.shape[0]

    planes = parts // 2
    share, columns = qkv_weight.shape
    fetch = []
    for p in range(parts):
        for e in range(experts):
            source = (e + p // 2 + 4 * (p % 2)) % experts
            fetch.append((p * experts + source, p * experts + e))
    w = lax.dynamic_slice(qkv_weight, (0, lax.rem(part, 2) * (columns // 2)), (share, columns // 2))
    w = lax.ppermute(w, ("dp", "expert"), fetch)

    pieces = (3, 1)
    outgoing = list(pack(kept_blocks[0], expert_out[0].reshape(slots, devices, quarter), experts, pieces))

    ids = jnp.concatenate([expert_ids, gate_levels], axis=1)
    ids, w = lax.optimization_barrier((ids, w))
    ids = lax.all_gather(ids, "tensor")
    weight = lax.all_gather(w, "dp", axis=0, tiled=True).reshape(planes, 2, share, columns // 2)
    sel = select(ids, experts, slots)
    sel, outgoing[1] = lax.optimization_barrier((sel, outgoing[1]))

    gain = norm_gain.astype(F32)
    inv_gain = (1.0 / gain).reshape(tensors, 1, quarter)
    own_gain = lax.dynamic_slice(gain, (quarter_of * quarter,), (quarter,)).reshape(1, quarter)
    place = jnp.concatenate(
        [mine[None], (quarter_of - jnp.arange(tensors, dtype=jnp.int32)) % tensors]
    ).astype(jnp.int32)

    exchanged = []
    first = 0
    for packed in outgoing:
        n = packed.shape[1]
        arrived = lax.all_to_all(packed, "expert", 0, 0, tiled=True)
        own = combine(sel, first, arrived, own_gain)
        exchanged.append(
            [own]
            + [
                lax.ppermute(own, "tensor", [(i, (i + k) % tensors) for i in range(tensors)])
                for k in range(1, tensors)
            ]
        )
        first += n
    return project(place, exchanged, weight, inv_gain)


def solution(mesh):
    in_specs = (
        P("expert", "dp", "tensor"),
        P("expert", "dp"),
        P(("dp", "expert", "tensor"), None),
        P(("dp", "expert", "tensor"), None),
        P(),
        P("expert", "tensor"),
    )
    out_specs = P(("dp", "expert"), "tensor")
    return jax.shard_map(local, mesh=mesh, in_specs=in_specs, out_specs=out_specs, check_vma=False)
```

```python
import functools

import jax
import jax.numpy as jnp
from jax import lax
from jax.experimental import pallas as pl
from jax.experimental.pallas import tpu as pltpu
from jax.sharding import PartitionSpec as P

F32 = jnp.float32
BF16 = jnp.bfloat16
VMEM_LIMIT = 60 * 1024 * 1024


def pack_kernel(tensors, first, kept_ref, rows_ref, out_ref):
    slots, owners, width = rows_ref.shape
    experts, count = out_ref.shape[:2]
    per_block = 4
    blocks = slots // per_block
    step = pl.program_id(0)
    row = lax.broadcasted_iota(jnp.int32, (experts * count * slots, 1), 0)
    slot, group = lax.rem(row, slots), lax.div(row, slots)
    owner = lax.div(group, count) * tensors + first + lax.rem(group, count)
    col = lax.broadcasted_iota(jnp.int32, (experts * count * slots, slots * owners), 1)
    move = (col == slot * owners + owner).astype(F32).astype(BF16)
    rows = [
        rows_ref[b * per_block : (b + 1) * per_block].reshape(per_block * owners, width)
        * (kept_ref[step * blocks + b] != 0).astype(F32).astype(BF16)
        for b in range(blocks)
    ]
    moved = jnp.dot(move, jnp.concatenate(rows, axis=0), preferred_element_type=F32)
    out_ref[...] = moved.astype(BF16).reshape(experts, count, slots, width)


def pack(kept, rows, experts, first, count):
    slots, owners, width = rows.shape
    step = 16
    return pl.pallas_call(
        functools.partial(pack_kernel, owners // experts, first),
        out_shape=jax.ShapeDtypeStruct((experts, count, slots, width), BF16),
        grid_spec=pltpu.PrefetchScalarGridSpec(
            num_scalar_prefetch=1,
            grid=(slots // step,),
            in_specs=[pl.BlockSpec((step, owners, width), lambda j, k: (j, 0, 0))],
            out_specs=pl.BlockSpec((experts, count, step, width), lambda j, k: (0, 0, j, 0)),
        ),
        compiler_params=pltpu.CompilerParams(vmem_limit_bytes=VMEM_LIMIT),
    )(kept, rows)


def select_kernel(experts, slots, ids_ref, sel_ref):
    tok = ids_ref.shape[1]
    cols = experts * slots
    row = lax.broadcasted_iota(jnp.int32, (tok, tok), 0)
    col = lax.broadcasted_iota(jnp.int32, (tok, tok), 1)
    before = (col < row).astype(F32).astype(BF16)
    lane = lax.broadcasted_iota(jnp.int32, (tok, 128), 1)
    place = lax.broadcasted_iota(jnp.int32, (tok, cols), 1)
    for q in range(ids_ref.shape[0]):
        both = ids_ref[q]
        hot = [(lane == both[:, k : k + 1]).astype(F32) for k in range(2)]
        earlier = jnp.dot(before, (hot[0] + hot[1]).astype(BF16), preferred_element_type=F32)
        total = jnp.zeros((tok, cols), F32)
        for k in range(2):
            slot = jnp.sum(earlier * hot[k], axis=1, keepdims=True).astype(jnp.int32)
            target = both[:, k : k + 1] * slots + slot
            share = both[:, 2 + k : 3 + k].astype(F32) / 256.0
            total = total + jnp.where(place == target, share, 0.0)
        sel_ref[q] = total.astype(BF16)


def select(ids, experts, slots):
    owners, tok, _ = ids.shape
    return pl.pallas_call(
        functools.partial(select_kernel, experts, slots),
        out_shape=jax.ShapeDtypeStruct((owners, tok, experts * slots), BF16),
    )(ids)


def combine_kernel(sel_ref, rows_ref, gain_ref, out_ref):
    experts, owners, slots, width = rows_ref.shape
    tok = sel_ref.shape[1]
    for q in range(owners):
        rows = rows_ref[:, q].reshape(experts * slots, width)
        total = jnp.dot(sel_ref[q], rows, preferred_element_type=F32)
        out_ref[pl.ds(q * tok, tok), :] = (total * gain_ref[...]).astype(BF16)


def combine(sel, first, rows, gain):
    tok, cols = sel.shape[1:]
    experts, owners, slots, width = rows.shape
    return pl.pallas_call(
        combine_kernel,
        out_shape=jax.ShapeDtypeStruct((owners * tok, width), BF16),
        grid=(1,),
        in_specs=[
            pl.BlockSpec((owners, tok, cols), lambda i: (first // owners, 0, 0)),
            pl.BlockSpec(rows.shape, lambda i: (0, 0, 0, 0)),
            pl.BlockSpec(gain.shape, lambda i: (0, 0)),
        ],
        out_specs=pl.BlockSpec((owners * tok, width), lambda i: (0, 0)),
        cost_estimate=pl.CostEstimate(flops=50_625_000_000, bytes_accessed=0, transcendentals=0),
        compiler_params=pltpu.CompilerParams(vmem_limit_bytes=VMEM_LIMIT),
    )(sel, rows, gain)


def project_kernel(width, place_ref, own_ref, one_ref, two_ref, three_ref, w_ref, inv_ref, *rest):
    out_ref, scale_ref = rest[-2:]
    blocks = (own_ref, one_ref, two_ref, three_ref)
    half = pl.program_id(0)

    @pl.when(half == 0)
    def _():
        total = jnp.zeros(scale_ref.shape, F32)
        for k, block in enumerate(blocks):
            plain = block[...].astype(F32) * inv_ref[place_ref[1 + k]]
            total = total + jnp.sum(plain * plain, axis=1, keepdims=True)
        scale_ref[...] = lax.rsqrt(total / width + 1e-05)

    shards, _, share, _ = w_ref.shape
    acc = None
    for k, block in enumerate(blocks):
        for i in range(2):
            shard = 2 * place_ref[1 + k] + i
            at = lax.rem(shard - place_ref[0] + 4 * half + shards, shards)
            term = jnp.dot(block[:, i * share : (i + 1) * share], w_ref[at, 0], preferred_element_type=F32)
            acc = term if acc is None else acc + term
    out_ref[...] = (acc * scale_ref[...]).astype(BF16)


def project(place, blocks, weight, inv_gain, total_rows, row_block, into=None):
    rows, quarter = blocks[0].shape
    shards, halves, share, columns = weight.shape
    whole = pl.BlockSpec((rows, quarter), lambda j, p: (0, 0))
    in_specs = [whole] * 4 + [
        pl.BlockSpec((shards, 1, share, columns), lambda j, p: (0, j, 0, 0)),
        pl.BlockSpec(inv_gain.shape, lambda j, p: (0, 0, 0)),
    ]
    args = [place, *blocks, weight, inv_gain]
    aliases = {}
    if into is not None:
        in_specs.append(pl.BlockSpec(memory_space=pl.ANY))
        aliases = {len(args): 0}
        args.append(into)
    return pl.pallas_call(
        functools.partial(project_kernel, 4 * quarter),
        out_shape=jax.ShapeDtypeStruct((total_rows, halves * columns), BF16),
        grid_spec=pltpu.PrefetchScalarGridSpec(
            num_scalar_prefetch=1,
            grid=(halves,),
            in_specs=in_specs,
            out_specs=pl.BlockSpec((rows, columns), lambda j, p: (row_block, j)),
            scratch_shapes=[pltpu.VMEM((rows, 1), F32)],
        ),
        input_output_aliases=aliases,
        compiler_params=pltpu.CompilerParams(vmem_limit_bytes=VMEM_LIMIT),
    )(*args)


def local(expert_out, kept_blocks, expert_ids, gate_levels, norm_gain, qkv_weight):
    parts = lax.axis_size("dp")
    experts = lax.axis_size("expert")
    tensors = lax.axis_size("tensor")
    part, mine, quarter_of = (lax.axis_index(a) for a in ("dp", "expert", "tensor"))
    devices = experts * tensors
    rows, quarter = expert_out.shape[1:]
    slots = rows // devices
    tok = expert_ids.shape[0]

    planes = parts // 2
    share, columns = qkv_weight.shape
    fetch = []
    for p in range(parts):
        for e in range(experts):
            source = (e + p // 2 + 4 * (p % 2)) % experts
            fetch.append((p * experts + source, p * experts + e))
    w = lax.dynamic_slice(qkv_weight, (0, lax.rem(part, 2) * (columns // 2)), (share, columns // 2))
    w = lax.ppermute(w, ("dp", "expert"), fetch)

    pieces = (2, 2)
    slotted = expert_out[0].reshape(slots, devices, quarter)
    outgoing = [pack(kept_blocks[0], slotted, experts, sum(pieces[:i]), n) for i, n in enumerate(pieces)]

    ids = jnp.concatenate([expert_ids, gate_levels], axis=1)
    ids, w = lax.optimization_barrier((ids, w))
    ids = lax.all_gather(ids, "tensor")
    weight = lax.all_gather(w, "dp", axis=0, tiled=True).reshape(planes, 2, share, columns // 2)
    sel = select(ids, experts, slots)
    sel, outgoing[1] = lax.optimization_barrier((sel, outgoing[1]))

    gain = norm_gain.astype(F32)
    inv_gain = (1.0 / gain).reshape(tensors, 1, quarter)
    own_gain = lax.dynamic_slice(gain, (quarter_of * quarter,), (quarter,)).reshape(1, quarter)
    place = jnp.concatenate(
        [mine[None], (quarter_of - jnp.arange(tensors, dtype=jnp.int32)) % tensors]
    ).astype(jnp.int32)

    out = None
    first = 0
    for packed in outgoing:
        n = packed.shape[1]
        arrived = lax.all_to_all(packed, "expert", 0, 0, tiled=True)
        own = combine(sel, first, arrived, own_gain)
        blocks = [own] + [
            lax.ppermute(own, "tensor", [(i, (i + k) % tensors) for i in range(tensors)])
            for k in range(1, tensors)
        ]
        out = project(place, blocks, weight, inv_gain, tensors * tok, first // n, out)
        first += n
    return out


def solution(mesh):
    in_specs = (
        P("expert", "dp", "tensor"),
        P("expert", "dp"),
        P(("dp", "expert", "tensor"), None),
        P(("dp", "expert", "tensor"), None),
        P(),
        P("expert", "tensor"),
    )
    out_specs = P(("dp", "expert"), "tensor")
    return jax.shard_map(local, mesh=mesh, in_specs=in_specs, out_specs=out_specs, check_vma=False)
```

```python
import functools

import jax
import jax.numpy as jnp
from jax import lax
from jax.experimental import pallas as pl
from jax.experimental.pallas import tpu as pltpu
from jax.sharding import PartitionSpec as P

F32 = jnp.float32
BF16 = jnp.bfloat16
VMEM_LIMIT = 60 * 1024 * 1024


def pack_kernel(tensors, first, kept_ref, rows_ref, out_ref):
    slots, owners, width = rows_ref.shape
    experts, count = out_ref.shape[:2]
    per_block = 4
    blocks = slots // per_block
    step = pl.program_id(0)
    row = lax.broadcasted_iota(jnp.int32, (experts * count * slots, 1), 0)
    slot, group = lax.rem(row, slots), lax.div(row, slots)
    owner = lax.div(group, count) * tensors + first + lax.rem(group, count)
    col = lax.broadcasted_iota(jnp.int32, (experts * count * slots, slots * owners), 1)
    move = (col == slot * owners + owner).astype(F32).astype(BF16)
    rows = [
        rows_ref[b * per_block : (b + 1) * per_block].reshape(per_block * owners, width)
        * (kept_ref[step * blocks + b] != 0).astype(F32).astype(BF16)
        for b in range(blocks)
    ]
    moved = jnp.dot(move, jnp.concatenate(rows, axis=0), preferred_element_type=F32)
    out_ref[...] = moved.astype(BF16).reshape(experts, count, slots, width)


def pack(kept, rows, experts, first, count):
    slots, owners, width = rows.shape
    step = 16
    return pl.pallas_call(
        functools.partial(pack_kernel, owners // experts, first),
        out_shape=jax.ShapeDtypeStruct((experts, count, slots, width), BF16),
        grid_spec=pltpu.PrefetchScalarGridSpec(
            num_scalar_prefetch=1,
            grid=(slots // step,),
            in_specs=[pl.BlockSpec((step, owners, width), lambda j, k: (j, 0, 0))],
            out_specs=pl.BlockSpec((experts, count, step, width), lambda j, k: (0, 0, j, 0)),
        ),
        compiler_params=pltpu.CompilerParams(vmem_limit_bytes=VMEM_LIMIT),
    )(kept, rows)


def select_kernel(experts, slots, ids_ref, sel_ref):
    tok = ids_ref.shape[1]
    cols = experts * slots
    row = lax.broadcasted_iota(jnp.int32, (tok, tok), 0)
    col = lax.broadcasted_iota(jnp.int32, (tok, tok), 1)
    before = (col < row).astype(F32).astype(BF16)
    lane = lax.broadcasted_iota(jnp.int32, (tok, 128), 1)
    place = lax.broadcasted_iota(jnp.int32, (tok, cols), 1)
    for q in range(ids_ref.shape[0]):
        both = ids_ref[q]
        hot = [(lane == both[:, k : k + 1]).astype(F32) for k in range(2)]
        earlier = jnp.dot(before, (hot[0] + hot[1]).astype(BF16), preferred_element_type=F32)
        total = jnp.zeros((tok, cols), F32)
        for k in range(2):
            slot = jnp.sum(earlier * hot[k], axis=1, keepdims=True).astype(jnp.int32)
            target = both[:, k : k + 1] * slots + slot
            share = both[:, 2 + k : 3 + k].astype(F32) / 256.0
            total = total + jnp.where(place == target, share, 0.0)
        sel_ref[q] = total.astype(BF16)


def select(ids, experts, slots):
    owners, tok, _ = ids.shape
    return pl.pallas_call(
        functools.partial(select_kernel, experts, slots),
        out_shape=jax.ShapeDtypeStruct((owners, tok, experts * slots), BF16),
    )(ids)


def combine_kernel(sel_ref, rows_ref, gain_ref, out_ref):
    experts, owners, slots, width = rows_ref.shape
    tok = sel_ref.shape[1]
    for q in range(owners):
        rows = rows_ref[:, q].reshape(experts * slots, width)
        total = jnp.dot(sel_ref[q], rows, preferred_element_type=F32)
        out_ref[pl.ds(q * tok, tok), :] = (total * gain_ref[...]).astype(BF16)


def combine(sel, first, rows, gain):
    tok, cols = sel.shape[1:]
    experts, owners, slots, width = rows.shape
    return pl.pallas_call(
        combine_kernel,
        out_shape=jax.ShapeDtypeStruct((owners * tok, width), BF16),
        grid=(1,),
        in_specs=[
            pl.BlockSpec((owners, tok, cols), lambda i: (first // owners, 0, 0)),
            pl.BlockSpec(rows.shape, lambda i: (0, 0, 0, 0)),
            pl.BlockSpec(gain.shape, lambda i: (0, 0)),
        ],
        out_specs=pl.BlockSpec((owners * tok, width), lambda i: (0, 0)),
        cost_estimate=pl.CostEstimate(flops=50500000000, bytes_accessed=0, transcendentals=0),
        compiler_params=pltpu.CompilerParams(vmem_limit_bytes=16 * 1024 * 1024),
    )(sel, rows, gain)


def project_kernel(width, place_ref, own_ref, one_ref, two_ref, three_ref, w_ref, inv_ref, *rest):
    out_ref, scale_ref = rest[-2:]
    blocks = (own_ref, one_ref, two_ref, three_ref)
    half = lax.div(pl.program_id(0), 2)

    @pl.when(pl.program_id(0) == 0)
    def _():
        total = jnp.zeros(scale_ref.shape, F32)
        for k, block in enumerate(blocks):
            plain = block[...].astype(F32) * inv_ref[place_ref[1 + k]]
            total = total + jnp.sum(plain * plain, axis=1, keepdims=True)
        scale_ref[...] = lax.rsqrt(total / width + 1e-05)

    shards, _, share, _ = w_ref.shape
    acc = None
    for k, block in enumerate(blocks):
        for i in range(2):
            shard = 2 * place_ref[1 + k] + i
            at = lax.rem(shard - place_ref[0] + 4 * half + shards, shards)
            term = jnp.dot(block[:, i * share : (i + 1) * share], w_ref[at, 0], preferred_element_type=F32)
            acc = term if acc is None else acc + term
    out_ref[...] = (acc * scale_ref[...]).astype(BF16)


def project(place, blocks, weight, inv_gain, total_rows, row_block, into=None):
    rows, quarter = blocks[0].shape
    shards, halves, share, columns = weight.shape
    whole = pl.BlockSpec((rows, quarter), lambda j, p: (0, 0))
    in_specs = [whole] * 4 + [
        pl.BlockSpec((shards, 1, share, columns // 2), lambda j, p: (0, j // 2, 0, j % 2)),
        pl.BlockSpec(inv_gain.shape, lambda j, p: (0, 0, 0)),
    ]
    args = [place, *blocks, weight, inv_gain]
    aliases = {}
    if into is not None:
        in_specs.append(pl.BlockSpec(memory_space=pl.ANY))
        aliases = {len(args): 0}
        args.append(into)
    return pl.pallas_call(
        functools.partial(project_kernel, 4 * quarter),
        out_shape=jax.ShapeDtypeStruct((total_rows, halves * columns), BF16),
        grid_spec=pltpu.PrefetchScalarGridSpec(
            num_scalar_prefetch=1,
            grid=(2 * halves,),
            in_specs=in_specs,
            out_specs=pl.BlockSpec((rows, columns // 2), lambda j, p: (row_block, j)),
            scratch_shapes=[pltpu.VMEM((rows, 1), F32)],
        ),
        input_output_aliases=aliases,
        compiler_params=pltpu.CompilerParams(vmem_limit_bytes=24 * 1024 * 1024),
    )(*args)


def local(expert_out, kept_blocks, expert_ids, gate_levels, norm_gain, qkv_weight):
    parts = lax.axis_size("dp")
    experts = lax.axis_size("expert")
    tensors = lax.axis_size("tensor")
    part, mine, quarter_of = (lax.axis_index(a) for a in ("dp", "expert", "tensor"))
    devices = experts * tensors
    rows, quarter = expert_out.shape[1:]
    slots = rows // devices
    tok = expert_ids.shape[0]

    planes = parts // 2
    share, columns = qkv_weight.shape
    fetch = []
    for p in range(parts):
        for e in range(experts):
            source = (e + p // 2 + 4 * (p % 2)) % experts
            fetch.append((p * experts + source, p * experts + e))
    w = lax.dynamic_slice(qkv_weight, (0, lax.rem(part, 2) * (columns // 2)), (share, columns // 2))
    w = lax.ppermute(w, ("dp", "expert"), fetch)

    pieces = (2, 2)
    slotted = expert_out[0].reshape(slots, devices, quarter)
    outgoing = [pack(kept_blocks[0], slotted, experts, sum(pieces[:i]), n) for i, n in enumerate(pieces)]

    ids = jnp.concatenate([expert_ids, gate_levels], axis=1)
    ids, w = lax.optimization_barrier((ids, w))
    ids = lax.all_gather(ids, "tensor")
    weight = lax.all_gather(w, "dp", axis=0, tiled=True).reshape(planes, 2, share, columns // 2)
    sel = select(ids, experts, slots)
    sel, outgoing[1] = lax.optimization_barrier((sel, outgoing[1]))

    gain = norm_gain.astype(F32)
    inv_gain = (1.0 / gain).reshape(tensors, 1, quarter)
    own_gain = lax.dynamic_slice(gain, (quarter_of * quarter,), (quarter,)).reshape(1, quarter)
    place = jnp.concatenate(
        [mine[None], (quarter_of - jnp.arange(tensors, dtype=jnp.int32)) % tensors]
    ).astype(jnp.int32)

    out = None
    first = 0
    for packed in outgoing:
        n = packed.shape[1]
        arrived = lax.all_to_all(packed, "expert", 0, 0, tiled=True)
        own = combine(sel, first, arrived, own_gain)
        blocks = [own] + [
            lax.ppermute(own, "tensor", [(i, (i + k) % tensors) for i in range(tensors)])
            for k in range(1, tensors)
        ]
        out = project(place, blocks, weight, inv_gain, tensors * tok, first // n, out)
        first += n
    return out


def solution(mesh):
    in_specs = (
        P("expert", "dp", "tensor"),
        P("expert", "dp"),
        P(("dp", "expert", "tensor"), None),
        P(("dp", "expert", "tensor"), None),
        P(),
        P("expert", "tensor"),
    )
    out_specs = P(("dp", "expert"), "tensor")
    return jax.shard_map(local, mesh=mesh, in_specs=in_specs, out_specs=out_specs, check_vma=False)
```

```python
import functools

import jax
import jax.numpy as jnp
from jax import lax
from jax.experimental import pallas as pl
from jax.experimental.pallas import tpu as pltpu
from jax.sharding import PartitionSpec as P

F32 = jnp.float32
BF16 = jnp.bfloat16
VMEM_LIMIT = 60 * 1024 * 1024


def pack_kernel(tensors, first, kept_ref, rows_ref, out_ref):
    slots, owners, width = rows_ref.shape
    experts, count = out_ref.shape[:2]
    per_block = 4
    blocks = slots // per_block
    step = pl.program_id(0)
    row = lax.broadcasted_iota(jnp.int32, (experts * count * slots, 1), 0)
    slot, group = lax.rem(row, slots), lax.div(row, slots)
    owner = lax.div(group, count) * tensors + first + lax.rem(group, count)
    col = lax.broadcasted_iota(jnp.int32, (experts * count * slots, slots * owners), 1)
    move = (col == slot * owners + owner).astype(F32).astype(BF16)
    rows = [
        rows_ref[b * per_block : (b + 1) * per_block].reshape(per_block * owners, width)
        * (kept_ref[step * blocks + b] != 0).astype(F32).astype(BF16)
        for b in range(blocks)
    ]
    moved = jnp.dot(move, jnp.concatenate(rows, axis=0), preferred_element_type=F32)
    out_ref[...] = moved.astype(BF16).reshape(experts, count, slots, width)


def pack(kept, rows, experts, first, count):
    slots, owners, width = rows.shape
    step = 16
    return pl.pallas_call(
        functools.partial(pack_kernel, owners // experts, first),
        out_shape=jax.ShapeDtypeStruct((experts, count, slots, width), BF16),
        grid_spec=pltpu.PrefetchScalarGridSpec(
            num_scalar_prefetch=1,
            grid=(slots // step,),
            in_specs=[pl.BlockSpec((step, owners, width), lambda j, k: (j, 0, 0))],
            out_specs=pl.BlockSpec((experts, count, step, width), lambda j, k: (0, 0, j, 0)),
        ),
        compiler_params=pltpu.CompilerParams(vmem_limit_bytes=VMEM_LIMIT),
    )(kept, rows)


def select_kernel(experts, slots, ids_ref, sel_ref):
    tok = ids_ref.shape[1]
    cols = experts * slots
    row = lax.broadcasted_iota(jnp.int32, (tok, tok), 0)
    col = lax.broadcasted_iota(jnp.int32, (tok, tok), 1)
    before = (col < row).astype(F32).astype(BF16)
    lane = lax.broadcasted_iota(jnp.int32, (tok, 128), 1)
    place = lax.broadcasted_iota(jnp.int32, (tok, cols), 1)
    for q in range(ids_ref.shape[0]):
        both = ids_ref[q]
        hot = [(lane == both[:, k : k + 1]).astype(F32) for k in range(2)]
        earlier = jnp.dot(before, (hot[0] + hot[1]).astype(BF16), preferred_element_type=F32)
        total = jnp.zeros((tok, cols), F32)
        for k in range(2):
            slot = jnp.sum(earlier * hot[k], axis=1, keepdims=True).astype(jnp.int32)
            target = both[:, k : k + 1] * slots + slot
            share = both[:, 2 + k : 3 + k].astype(F32) / 256.0
            total = total + jnp.where(place == target, share, 0.0)
        sel_ref[q] = total.astype(BF16)


def select(ids, experts, slots):
    owners, tok, _ = ids.shape
    return pl.pallas_call(
        functools.partial(select_kernel, experts, slots),
        out_shape=jax.ShapeDtypeStruct((owners, tok, experts * slots), BF16),
        compiler_params=pltpu.CompilerParams(vmem_limit_bytes=16 * 1024 * 1024),
    )(ids)


def combine_kernel(sel_ref, rows_ref, gain_ref, out_ref):
    experts, owners, slots, width = rows_ref.shape
    tok = sel_ref.shape[1]
    for q in range(owners):
        rows = rows_ref[:, q].reshape(experts * slots, width)
        total = jnp.dot(sel_ref[q], rows, preferred_element_type=F32)
        out_ref[pl.ds(q * tok, tok), :] = (total * gain_ref[...]).astype(BF16)


def combine(sel, first, rows, gain):
    tok, cols = sel.shape[1:]
    experts, owners, slots, width = rows.shape
    return pl.pallas_call(
        combine_kernel,
        out_shape=jax.ShapeDtypeStruct((owners * tok, width), BF16),
        grid=(1,),
        in_specs=[
            pl.BlockSpec((owners, tok, cols), lambda i: (first // owners, 0, 0)),
            pl.BlockSpec(rows.shape, lambda i: (0, 0, 0, 0)),
            pl.BlockSpec(gain.shape, lambda i: (0, 0)),
        ],
        out_specs=pl.BlockSpec((owners * tok, width), lambda i: (0, 0)),
        cost_estimate=pl.CostEstimate(flops=50500000000, bytes_accessed=0, transcendentals=0),
        compiler_params=pltpu.CompilerParams(vmem_limit_bytes=16 * 1024 * 1024),
    )(sel, rows, gain)


def project_kernel(width, place_ref, own_ref, two_ref, one_ref, three_ref, w_ref, inv_ref, *rest):
    out_ref, scale_ref = rest[-2:]
    blocks = (own_ref, two_ref, one_ref, three_ref)
    half = lax.div(pl.program_id(0), 2)

    @pl.when(pl.program_id(0) == 0)
    def _():
        total = jnp.zeros(scale_ref.shape, F32)
        for k, block in enumerate(blocks):
            plain = block[...].astype(F32) * inv_ref[place_ref[1 + k]]
            total = total + jnp.sum(plain * plain, axis=1, keepdims=True)
        scale_ref[...] = lax.rsqrt(total / width + 1e-05)

    shards, _, share, _ = w_ref.shape
    acc = None
    for k, block in enumerate(blocks):
        for i in range(2):
            shard = 2 * place_ref[1 + k] + i
            at = lax.rem(shard - place_ref[0] + 4 * half + shards, shards)
            term = jnp.dot(block[:, i * share : (i + 1) * share], w_ref[at, 0], preferred_element_type=F32)
            acc = term if acc is None else acc + term
    out_ref[...] = (acc * scale_ref[...]).astype(BF16)


def project(place, blocks, weight, inv_gain, total_rows, row_block, into=None):
    rows, quarter = blocks[0].shape
    shards, halves, share, columns = weight.shape
    whole = pl.BlockSpec((rows, quarter), lambda j, p: (0, 0))
    in_specs = [whole] * 4 + [
        pl.BlockSpec((shards, 1, share, columns // 2), lambda j, p: (0, j // 2, 0, j % 2)),
        pl.BlockSpec(inv_gain.shape, lambda j, p: (0, 0, 0)),
    ]
    args = [place, *blocks, weight, inv_gain]
    aliases = {}
    if into is not None:
        in_specs.append(pl.BlockSpec(memory_space=pl.ANY))
        aliases = {len(args): 0}
        args.append(into)
    return pl.pallas_call(
        functools.partial(project_kernel, 4 * quarter),
        out_shape=jax.ShapeDtypeStruct((total_rows, halves * columns), BF16),
        grid_spec=pltpu.PrefetchScalarGridSpec(
            num_scalar_prefetch=1,
            grid=(2 * halves,),
            in_specs=in_specs,
            out_specs=pl.BlockSpec((rows, columns // 2), lambda j, p: (row_block, j)),
            scratch_shapes=[pltpu.VMEM((rows, 1), F32)],
        ),
        input_output_aliases=aliases,
        compiler_params=pltpu.CompilerParams(vmem_limit_bytes=24 * 1024 * 1024),
    )(*args)


def local(expert_out, kept_blocks, expert_ids, gate_levels, norm_gain, qkv_weight):
    parts = lax.axis_size("dp")
    experts = lax.axis_size("expert")
    tensors = lax.axis_size("tensor")
    part, mine, quarter_of = (lax.axis_index(a) for a in ("dp", "expert", "tensor"))
    devices = experts * tensors
    rows, quarter = expert_out.shape[1:]
    slots = rows // devices
    tok = expert_ids.shape[0]

    planes = parts // 2
    share, columns = qkv_weight.shape
    fetch = []
    for p in range(parts):
        for e in range(experts):
            source = (e + p // 2 + 4 * (p % 2)) % experts
            fetch.append((p * experts + source, p * experts + e))
    w = lax.dynamic_slice(qkv_weight, (0, lax.rem(part, 2) * (columns // 2)), (share, columns // 2))
    w = lax.ppermute(w, ("dp", "expert"), fetch)

    pieces = (2, 2)
    slotted = expert_out[0].reshape(slots, devices, quarter)
    outgoing = [pack(kept_blocks[0], slotted, experts, sum(pieces[:i]), n) for i, n in enumerate(pieces)]

    ids = jnp.concatenate([expert_ids, gate_levels], axis=1)
    ids, w = lax.optimization_barrier((ids, w))
    ids = lax.all_gather(ids, "tensor")
    weight = lax.all_gather(w, "dp", axis=0, tiled=True).reshape(planes, 2, share, columns // 2)
    sel = select(ids, experts, slots)
    sel, outgoing[1] = lax.optimization_barrier((sel, outgoing[1]))

    gain = norm_gain.astype(F32)
    inv_gain = (1.0 / gain).reshape(tensors, 1, quarter)
    own_gain = lax.dynamic_slice(gain, (quarter_of * quarter,), (quarter,)).reshape(1, quarter)
    place = jnp.concatenate(
        [mine[None], (quarter_of - jnp.array([0, 2, 1, 3], dtype=jnp.int32)) % tensors]
    ).astype(jnp.int32)

    out = None
    first = 0
    for packed in outgoing:
        n = packed.shape[1]
        arrived = lax.all_to_all(packed, "expert", 0, 0, tiled=True)
        own = combine(sel, first, arrived, own_gain)
        sent = {
            k: lax.ppermute(own, "tensor", [(i, (i + k) % tensors) for i in range(tensors)])
            for k in (2, 1, 3)
        }
        blocks = [own, sent[2], sent[1], sent[3]]
        out = project(place, blocks, weight, inv_gain, tensors * tok, first // n, out)
        first += n
    return out


def solution(mesh):
    in_specs = (
        P("expert", "dp", "tensor"),
        P("expert", "dp"),
        P(("dp", "expert", "tensor"), None),
        P(("dp", "expert", "tensor"), None),
        P(),
        P("expert", "tensor"),
    )
    out_specs = P(("dp", "expert"), "tensor")
    return jax.shard_map(local, mesh=mesh, in_specs=in_specs, out_specs=out_specs, check_vma=False)
```
